256 devices in a mesh: row: 16 (over x, z_lo, core), col: 16 (over y, z_hi).
Axes of the slice: x: 4, y: 4, z: 8 (z_hi: 4, z_lo: 2; z = z_hi * 2 + z_lo), core: 2. Of those that a mesh axis runs over, the one named last changes fastest.
Arguments:
- amplitudes: bfloat16 [9984, 4096], P('row', 'col'), may hold values from -6 to 6
- tiles: bfloat16 [16, 128, 128, 128], P('col', 'row'), may hold values from -0.09375 to 0.09375
- tile_ids: int32 [16, 128], P('col', 'row'), may hold values from -1 to 511, as said below
Outputs:
- ladder: bfloat16 [9984, 32768], P('row', 'col')
The draws below stay inside these ranges and needn't reach their ends.
Inputs may be any that keep to these rules, and one draw needn't show every extreme that they name: `tile_ids`: within one grid column the non-negative ids are distinct; in every column one device's block of 8 slots is all live, and within each device's block live slots come first.
All inputs are finite; a program needn't handle non-finite values.
Results may differ from the reference program's by a relative error of at most 0.001.
Values may be sent and summed in bfloat16 or wider, within the bound.
No kernel may reach another device: no remote copies, remote signals or barrier semaphores. Data moves between devices by JAX's collectives and lax.ppermute only.
A program may use at most 128 MiB of HBM per device.

```python
import jax
import jax.numpy as jnp
from jax import lax

TILE = 128
KT = 32
NQ = 16
SLOTS = 8
ROWS = 9984
K = 4096
COL_SLOTS = 128
N_ROW = 16
N_COL = 16


def draw_tile_ids(key, part):
    key = jax.random.fold_in(key, 11)

    def one_column(column_key):
        perm_key, count_key, full_key = jax.random.split(column_key, 3)
        order = jax.random.permutation(perm_key, KT * NQ)[:N_ROW * SLOTS]
        counts = jax.random.randint(count_key, (N_ROW,), SLOTS // 2, SLOTS + 1)
        full_owner = jax.random.randint(full_key, (), 0, N_ROW)
        counts = jnp.where(jnp.arange(N_ROW) == full_owner, SLOTS, counts)
        live = jnp.arange(SLOTS)[None, :] < counts[:, None]
        return jnp.where(live.reshape(-1), order, -1).astype(jnp.int32)
    return jax.vmap(one_column)(jax.random.split(key, N_COL))


def steps_of(rng, shape, cuts, low, top_value):
    gain = 1.0
    for dim, shards_of in cuts:
        draws = jax.random.uniform(jax.random.fold_in(jax.random.fold_in(rng, 6), dim), (shards_of,), jnp.float32, low / len(cuts), top_value / len(cuts))
        gain = gain * jnp.repeat(jnp.exp(draws), shape[dim] // shards_of).reshape((-1,) + (1,) * (len(shape) - 1 - dim))
    return gain


def scatter_about(own_key, dims, spread, limit, pieces=(), kind=jnp.bfloat16):
    result = spread * jax.random.normal(own_key, dims, jnp.float32)
    if pieces:
        result = result * steps_of(own_key, dims, pieces, -0.22, 0.18)
    return jnp.clip(result, -limit, limit).astype(kind)


def setup_inputs(seed: int = 0) -> dict:
    arg_keys = jax.random.split(jax.random.key(seed), 4)
    amplitudes = scatter_about(arg_keys[0], (ROWS, K), 1.0, 6.0, ((0, 16), (1, 16)))
    tiles = scatter_about(arg_keys[1], (N_COL, COL_SLOTS, TILE, TILE), K ** -0.5, 0.09375, ((0, 16), (1, 16)))
    tile_ids = draw_tile_ids(jax.random.fold_in(arg_keys[3], 71), 0)
    return {"amplitudes": amplitudes, "tiles": tiles, "tile_ids": tile_ids}


def column_block(pair):
    column_tiles, column_ids = pair
    index = jnp.where(column_ids >= 0, column_ids, KT * NQ).astype(jnp.int32)
    dense = jnp.zeros((KT * NQ + 1, TILE, TILE), column_tiles.dtype).at[index].set(column_tiles)
    dense = dense[: KT * NQ].reshape(KT, NQ, TILE, TILE).transpose(0, 2, 1, 3).reshape(KT * TILE, NQ * TILE)
    return dense


def reference(amplitudes, tiles, tile_ids):
    def one_column(pair):
        dense = column_block(pair)
        return jnp.dot(amplitudes, dense, preferred_element_type=jnp.float32).astype(jnp.bfloat16)

    blocks = lax.map(one_column, (tiles, tile_ids))
    return blocks.transpose(1, 0, 2).reshape(amplitudes.shape[0], -1)
```

```python
import functools
import itertools

import jax
import jax.numpy as jnp
from jax import lax
from jax.experimental import pallas as pl
from jax.experimental.pallas import tpu as pltpu
from jax.sharding import PartitionSpec as P

TILE = 128
NQ = 16
ROWS = 624
ROWS_A = 480
ROWS_B = ROWS - ROWS_A
HALF = 320
HALF_A = ROWS_A // 2
SLOTS = 8
HELD = 64
EARLY_SLOTS = 48
EARLY = (0, 1, 2, 3, 4, 5, 6, 8, 9, 10)
GROUP = 4
PAIR = 2
STEPS = NQ // PAIR
WIDTH = TILE * PAIR


def rank_of(d):
    return d ^ (d >> 1)


def fence(*values):
    return lax.optimization_barrier(values)


def from_col(value, dy=0, dz=0):
    perm = [
        ((y + dy) % 4 * 4 + (z + dz) % 4, y * 4 + z) for y in range(4) for z in range(4)
    ]
    return lax.ppermute(value, "col", perm)


def from_row(value, dx=0, dz=0, dcore=0):
    perm = []
    for x, z, core in itertools.product(range(4), range(2), range(2)):
        at_x = (x + dx * (1 - 2 * core)) % 4
        perm.append(((at_x * 2 + (z ^ dz)) * 2 + (core ^ dcore), (x * 2 + z) * 2 + core))
    return lax.ppermute(value, "row", perm)


def sort_tiles(position, tiles, wanted, codes, codes_smem, lists, counts, sem):
    n = tiles.shape[0]
    y, z = position[0], position[1]
    lane = lax.broadcasted_iota(jnp.int32, (1, TILE), 1)
    for i in range(n):
        rows = tiles[i, SLOTS * TILE : SLOTS * TILE + 16, :].astype(jnp.float32)
        kt, qt = rows[0:1].astype(jnp.int32), rows[1:2].astype(jnp.int32)
        owner = kt >> 1
        place = rank_of(((owner & 3) - z) & 3) * 4 + rank_of(((owner >> 2) - y) & 3)
        block = (place * 2 + (kt & 1)) & 31
        live = (kt >= 0) & wanted(i * SLOTS + lane, block)
        codes[i : i + 1, :] = jnp.where(live, (qt & 15) * 32 + block, NQ * 32)
    copy = pltpu.make_async_copy(codes, codes_smem, sem)
    copy.start()
    for q in range(NQ + 1):
        counts[q] = 0
    copy.wait()

    def put(i, carry):
        for j in range(SLOTS):
            code = codes_smem[i, j]
            q = code >> 5
            at = counts[q]
            lists[q * 32 + at] = (i * SLOTS + j) * 32 + (code & 31)
            counts[q] = at + 1
        return carry

    lax.fori_loop(0, n, put, 0)


def products(lists, counts, tiles, amps, step):
    groups, functions = [], []
    for i in range(PAIR):
        q = step * PAIR + i
        count = counts[q]

        def product(group, q=q, count=count):
            left, right = [], []
            for j in range(GROUP):
                at = group * GROUP + j
                live = at < count
                item = jnp.where(live, lists[q * 32 + jnp.minimum(at, 31)], 0)
                slot = item >> 5
                row = pl.ds(pl.multiple_of((slot & 7) * TILE, TILE), TILE)
                tile = tiles[slot >> 3, row, :]
                right.append(jnp.where(live, tile, jnp.zeros_like(tile)))
                left.append(amps[item & 31])
            return jnp.dot(
                jnp.concatenate(left, axis=1),
                jnp.concatenate(right, axis=0),
                preferred_element_type=jnp.float32,
            )

        groups.append((count + GROUP - 1) // GROUP)
        functions.append(product)
    return functools.reduce(jnp.maximum, groups), functions


def accumulate(lists, counts, tiles, amps, step, before, total):
    groups, functions = products(lists, counts, tiles, amps, step)
    for i, value in enumerate([function(0) for function in functions]):
        part = slice(i * TILE, (i + 1) * TILE)
        total[:, part] = value if before is None else before[:, part] + value

    def more(group, carry):
        for i, value in enumerate([function(group) for function in functions]):
            total[:, i * TILE : (i + 1) * TILE] += value
        return carry

    lax.fori_loop(1, groups, more, 0)


def moves(plan, pieces, amps, sem):
    return [
        pltpu.make_async_copy(
            pieces[ref].at[pl.ds(src, rows), pl.ds(sub * TILE, TILE)],
            amps.at[place * 2 + sub, pl.ds(dst, rows)],
            sem,
        )
        for ref, src, rows, place, dst in plan
        for sub in range(2)
    ]


def early_pair(slot, block):
    early = functools.reduce(jnp.logical_or, [(block >> 1) == place for place in EARLY])
    return (slot < EARLY_SLOTS) & early


def first_part(plan, n_pieces, position, tiles, *refs):
    amps, partial, codes, codes_smem, lists, counts, sem, code_sem = refs[n_pieces:]
    copies = moves(plan, refs[:n_pieces], amps, sem)
    for copy in copies:
        copy.start()
    sort_tiles(position, tiles, early_pair, codes, codes_smem, lists, counts, code_sem)
    for copy in copies:
        copy.wait()

    @pl.loop(0, STEPS)
    def _(step):
        accumulate(lists, counts, tiles, amps, step, None, partial.at[step])


def second_part(plan, n_pieces, position, tiles, before_amps, before, *refs):
    amps, partial, codes, codes_smem, lists, counts, sem, code_sem = refs[n_pieces:]
    copies = moves(plan, refs[:n_pieces], amps, sem)
    for copy in copies:
        copy.start()
    sort_tiles(
        position, tiles, lambda slot, block: jnp.logical_not(early_pair(slot, block)),
        codes, codes_smem, lists, counts, code_sem,
    )
    for copy in copies:
        copy.wait()

    @pl.loop(0, STEPS)
    def _(step):
        accumulate(lists, counts, tiles, amps, step, before.at[step], partial.at[step])


def last_part(position, tiles, amps, before, out, codes, codes_smem, lists, counts, total, stage, code_sem, out_sem):
    sort_tiles(
        position, tiles, lambda slot, block: slot >= 0, codes, codes_smem, lists, counts, code_sem
    )

    def write(step, slot):
        columns = pl.ds(pl.multiple_of(step * WIDTH, WIDTH), WIDTH)
        return pltpu.make_async_copy(stage.at[slot], out.at[:, columns], out_sem.at[slot])

    @pl.loop(0, STEPS)
    def _(step):
        slot = lax.rem(step, 2)

        @pl.when(step >= 2)
        def _():
            write(step - 2, slot).wait()

        accumulate(lists, counts, tiles, amps, step, before.at[step], total)
        stage[slot] = total[...].astype(jnp.bfloat16)
        write(step, slot).start()

    for step in range(STEPS - 2, STEPS):
        write(step, step % 2).wait()


def call(body, out_shape, out_specs, arguments, scratch, name, aliases={}):
    sorting = [
        pltpu.VMEM((8, TILE), jnp.int32),
        pltpu.SMEM((8, TILE), jnp.int32),
        pltpu.SMEM((NQ * 32 + HELD,), jnp.int32),
        pltpu.SMEM((NQ + 1,), jnp.int32),
    ]
    return pl.pallas_call(
        body,
        out_shape=out_shape,
        in_specs=[pl.BlockSpec(memory_space=space) for _, space in arguments],
        out_specs=out_specs,
        scratch_shapes=sorting + scratch,
        input_output_aliases=aliases,
        compiler_params=pltpu.CompilerParams(vmem_limit_bytes=24 * 2**20),
        cost_estimate=pl.CostEstimate(
            flops=5_000_000_000, bytes_accessed=16_000_000, transcendentals=0
        ),
        name=name,
    )(*(array for array, _ in arguments))


def chosen_part(plan, arrays, chosen, space):
    steps = [step for step in plan if step[0] in chosen]
    return [(step[0] - chosen[0],) + step[1:] for step in steps], [(arrays[i], space) for i in chosen]


IN_VMEM = pl.BlockSpec(memory_space=pltpu.VMEM)
SUMS = [
    jax.ShapeDtypeStruct((32, ROWS, TILE), jnp.bfloat16),
    jax.ShapeDtypeStruct((STEPS, ROWS, WIDTH), jnp.float32),
]


def contract_early(position, tiles, steps, pieces):
    return call(
        functools.partial(first_part, steps, len(pieces)),
        SUMS, [IN_VMEM, IN_VMEM],
        [(position, pltpu.SMEM), (tiles, pltpu.VMEM)] + pieces,
        [pltpu.SemaphoreType.DMA] * 2, "first_part",
    )


def contract_late(position, own, other, amps, partial, steps, pieces):
    smem, vmem, dma = pltpu.SMEM, pltpu.VMEM, pltpu.SemaphoreType.DMA
    amps, partial = call(
        functools.partial(second_part, steps, len(pieces)),
        SUMS, [IN_VMEM, IN_VMEM],
        [(position, smem), (own, vmem), (amps, vmem), (partial, vmem)] + pieces,
        [dma, dma], "second_part", {2: 0, 3: 1},
    )
    return call(
        last_part,
        jax.ShapeDtypeStruct((ROWS, NQ * TILE), jnp.bfloat16),
        pl.BlockSpec(memory_space=pl.ANY),
        [(position, smem), (other, vmem), (amps, vmem), (partial, vmem)],
        [pltpu.VMEM((ROWS, WIDTH), jnp.float32), pltpu.VMEM((2, ROWS, WIDTH), jnp.bfloat16), dma, dma((2,))],
        "last_part",
    )


def touch(*arrays):
    anywhere = pl.BlockSpec(memory_space=pl.ANY)
    return pl.pallas_call(
        lambda *refs: None,
        out_shape=[jax.ShapeDtypeStruct(array.shape, array.dtype) for array in arrays],
        in_specs=[anywhere] * len(arrays),
        out_specs=[anywhere] * len(arrays),
        input_output_aliases={i: i for i in range(len(arrays))},
        cost_estimate=pl.CostEstimate(
            flops=10_000_000_000, bytes_accessed=1_000_000, transcendentals=0
        ),
        name="touch",
    )(*arrays)


def shards(amplitudes, tiles, tile_ids):
    kt = jnp.where(tile_ids >= 0, tile_ids >> 4, -1)
    qt = tile_ids & 15
    ids = jnp.concatenate([kt, qt], axis=0).astype(jnp.bfloat16)
    ids = jnp.pad(ids, ((0, 14), (0, TILE - SLOTS)))
    block = jnp.concatenate([tiles.reshape(SLOTS * TILE, TILE), ids], axis=0)

    block_z = from_row(block, dz=1)
    y_up, y_down = (from_col(amplitudes, dy=dy) for dy in (1, 3))
    first = amplitudes[:ROWS_A]
    z_up, z_down = (from_col(first, dz=dz) for dz in (1, 3))
    z_up, z_down = touch(z_up, z_down)
    block_z, y_up, y_down, z_up, z_down = fence(block_z, y_up, y_down, z_up, z_down)

    x_blocks = [jnp.stack([block, block_z])]
    x_blocks.append(from_row(x_blocks[-1], dx=1))
    y_top, y_low = from_col(y_down[:HALF], dy=3), from_col(y_up[HALF:], dy=1)
    z_top, z_low = from_col(z_down[:HALF_A], dz=3), from_col(z_up[HALF_A:], dz=1)
    x_blocks[-1], y_top, y_low, z_top, z_low = fence(x_blocks[-1], y_top, y_low, z_top, z_low)

    firsts = [jnp.concatenate([z_up, z_down, z_top, z_low], axis=0)]
    lasts = [jnp.concatenate([rows[ROWS_A:] for rows in (amplitudes, y_up, y_down)] + [y_low[ROWS_A - HALF :]], axis=0)]
    x_blocks.append(from_row(x_blocks[-1], dx=1))
    firsts += [from_col(firsts[0], dy=dy) for dy in (1, 3)]
    lasts += [from_col(lasts[0], dz=dz) for dz in (1, 3)]
    x_blocks[-1], firsts[1], firsts[2], lasts[1], lasts[2] = fence(
        x_blocks[-1], firsts[1], firsts[2], lasts[1], lasts[2]
    )

    plan = [(0, 0, ROWS, 0, 0), (1, 0, ROWS, 1, 0), (2, 0, ROWS, 2, 0), (3, 0, HALF, 3, 0)]
    plan.append((4, 0, ROWS - HALF, 3, HALF))
    for i in range(3):
        for j in range(3):
            plan.append((5 + i, j * ROWS_A, ROWS_A, 4 * (j + 1) + i, 0))
    plan += [(10, 0, ROWS_A, 7, 0), (10, ROWS_A, HALF_A, 11, 0)]
    plan += [(11, 0, HALF_A, 11, HALF_A), (11, HALF_A, ROWS_A, 15, 0)]
    for j in range(4):
        plan.append((8, j * ROWS_B, ROWS_B, 4 + j, ROWS_A))
        plan.append((9, j * ROWS_B, ROWS_B, 8 + j, ROWS_A))
        plan.append((12 + j // 2, j % 2 * ROWS_B, ROWS_B, 12 + j, ROWS_A))
    cut, cut_b = 3 * ROWS_A // 2, 2 * ROWS_B
    early_tiles = jnp.concatenate(x_blocks, axis=0)
    x_blocks.append(from_row(x_blocks[-1], dx=1))
    firsts += [from_col(firsts[2][:cut], dy=3), from_col(firsts[1][cut:], dy=1)]
    lasts += [from_col(lasts[2][:cut_b], dz=3), from_col(lasts[1][cut_b:], dz=1)]
    position = jnp.stack([lax.axis_index("col") // 4, lax.axis_index("col") % 4]).astype(jnp.int32)
    arrays = [amplitudes, y_up, y_down, y_top, y_low] + firsts[:3] + lasts[1:3] + firsts[3:] + lasts[3:]
    amps, partial = contract_early(
        position, early_tiles, *chosen_part(plan, arrays, range(10), pl.ANY)
    )
    x_blocks[-1], amps, partial, *arrays[10:] = fence(x_blocks[-1], amps, partial, *arrays[10:])

    own = jnp.concatenate(x_blocks, axis=0)
    other = from_row(own, dcore=1)
    late = chosen_part(plan, arrays, range(10, 14), pltpu.HBM)
    return contract_late(position, own, other, amps, partial, *late)


def solution(mesh):
    in_specs = (P("row", "col"), P("col", "row", None, None), P("col", "row"))
    out_specs = P("row", "col")
    return jax.shard_map(shards, mesh=mesh, in_specs=in_specs, out_specs=out_specs, check_vma=False)
```

```python
import functools
import itertools

import jax
import jax.numpy as jnp
from jax import lax
from jax.experimental import pallas as pl
from jax.experimental.pallas import tpu as pltpu
from jax.sharding import PartitionSpec as P

TILE = 128
NQ = 16
ROWS = 624
ROWS_A = 480
ROWS_B = ROWS - ROWS_A
HALF = 320
HALF_A = ROWS_A // 2
SLOTS = 8
HELD = 64
EARLY_SLOTS = 48
EARLY = (0, 1, 2, 3, 4, 5, 6, 8, 9, 10)
BATCH = 6
SPAN = 4
EMPTY = -1


def rank_of(d):
    return d ^ (d >> 1)


def fence(*values):
    return lax.optimization_barrier(values)


def from_col(value, dy=0, dz=0):
    perm = [
        ((y + dy) % 4 * 4 + (z + dz) % 4, y * 4 + z) for y in range(4) for z in range(4)
    ]
    return lax.ppermute(value, "col", perm)


def from_row(value, dx=0, dz=0, dcore=0):
    perm = []
    for x, z, core in itertools.product(range(4), range(2), range(2)):
        at_x = (x + dx * (1 - 2 * core)) % 4
        perm.append(((at_x * 2 + (z ^ dz)) * 2 + (core ^ dcore), (x * 2 + z) * 2 + core))
    return lax.ppermute(value, "row", perm)


def pair_tiles(position, tiles, wanted, codes, codes_smem, pairs, last, counts, sem):
    n = tiles.shape[0]
    y, z = position[0], position[1]
    lane = lax.broadcasted_iota(jnp.int32, (1, TILE), 1)
    for i in range(n):
        rows = tiles[i, SLOTS * TILE : SLOTS * TILE + 16, :].astype(jnp.float32)
        kt, qt = rows[0:1].astype(jnp.int32), rows[1:2].astype(jnp.int32)
        owner = kt >> 1
        place = rank_of(((owner & 3) - z) & 3) * 4 + rank_of(((owner >> 2) - y) & 3)
        block = (place * 2 + (kt & 1)) & 31
        slot = i * SLOTS + lane
        live = (kt >= 0) & wanted(slot, block)
        codes[i : i + 1, :] = jnp.where(live, ((qt & 15) * HELD + slot) * 32 + block, EMPTY)
    copy = pltpu.make_async_copy(codes, codes_smem, sem)
    copy.start()
    for q in range(NQ + 1):
        counts[q] = 0
    copy.wait()

    def put(i, n_pairs):
        for j in range(SLOTS):
            code = codes_smem[i, j]
            live = code >= 0
            q = jnp.where(live, code >> 11, NQ)
            count = counts[q]
            opens = (count & 1) == 0
            at = jnp.where(live, jnp.where(opens, n_pairs, last[q]), HELD + BATCH)
            counts[q] = count + 1
            last[q] = at
            pairs[at * 2] = jnp.where(opens, code, pairs[at * 2])
            pairs[at * 2 + 1] = jnp.where(opens, EMPTY, code)
            n_pairs = n_pairs + (live & opens).astype(jnp.int32)
        return n_pairs

    for q in range(NQ + 1):
        last[q] = 0
    n_pairs = lax.fori_loop(0, n, put, jnp.int32(0))
    for i in range(2 * BATCH):
        pairs[n_pairs * 2 + i] = EMPTY
    return n_pairs


def accumulate(n_pairs, pairs, tiles, amps, sums):
    def load(code):
        item = jnp.maximum(code, 0)
        slot = (item >> 5) & (HELD - 1)
        row = pl.ds(pl.multiple_of((slot & 7) * TILE, TILE), TILE)
        tile = tiles[slot >> 3, row, :]
        return amps[item & 31], jnp.where(code >= 0, tile, jnp.zeros_like(tile))

    def step(batch, carry):
        values = []
        for i in range(BATCH):
            at = (batch * BATCH + i) * 2
            (left, upper), (right, lower) = load(pairs[at]), load(pairs[at + 1])
            value = jnp.dot(
                jnp.concatenate([left, right], axis=1),
                jnp.concatenate([upper, lower], axis=0),
                preferred_element_type=jnp.float32,
            )
            values.append((jnp.maximum(pairs[at], 0) >> 11, value))
        for q, value in values:
            sums[q] += value
        return carry

    lax.fori_loop(0, (n_pairs + BATCH - 1) // BATCH, step, 0)


def moves(plan, pieces, amps, sem):
    return [
        pltpu.make_async_copy(
            pieces[ref].at[pl.ds(src, rows), pl.ds(sub * TILE, TILE)],
            amps.at[place * 2 + sub, pl.ds(dst, rows)],
            sem,
        )
        for ref, src, rows, place, dst in plan
        for sub in range(2)
    ]


def early_pair(slot, block):
    early = functools.reduce(jnp.logical_or, [(block >> 1) == place for place in EARLY])
    return (slot < EARLY_SLOTS) & early


def first_part(plan, n_pieces, position, tiles, *refs):
    sums, *pairing, code_sem, sem, amps = refs[n_pieces:]
    copies = moves(plan, refs[:n_pieces], amps, sem)
    for copy in copies:
        copy.start()
    sums[...] = jnp.zeros_like(sums)
    n_pairs = pair_tiles(position, tiles, early_pair, *pairing, code_sem)
    for copy in copies:
        copy.wait()
    accumulate(n_pairs, pairing[2], tiles, amps, sums)


def second_part(plan, n_pieces, position, tiles, *refs):
    amps, sums, *pairing, code_sem, sem = refs[n_pieces:]
    copies = moves(plan, refs[:n_pieces], amps, sem)
    for copy in copies:
        copy.start()
    sums[...] = jnp.zeros_like(sums)

    def wanted(slot, block):
        return jnp.logical_not(early_pair(slot, block))

    n_pairs = pair_tiles(position, tiles, wanted, *pairing, code_sem)
    for copy in copies:
        copy.wait()
    accumulate(n_pairs, pairing[2], tiles, amps, sums)


def last_part(position, tiles, amps, first_sums, second_sums, out, *refs):
    *pairing, code_sem, sums, stage, out_sem = refs
    sums[...] = first_sums[...] + second_sums[...]
    n_pairs = pair_tiles(position, tiles, lambda slot, block: slot >= 0, *pairing, code_sem)
    accumulate(n_pairs, pairing[2], tiles, amps, sums)
    writes = []
    for i in range(NQ // SPAN):
        for j in range(SPAN):
            stage[i, :, j * TILE : (j + 1) * TILE] = sums[i * SPAN + j].astype(jnp.bfloat16)
        columns = pl.ds(i * SPAN * TILE, SPAN * TILE)
        writes.append(pltpu.make_async_copy(stage.at[i], out.at[:, columns], out_sem.at[i]))
        writes[i].start()
    for write in writes:
        write.wait()


def call(body, out_shape, out_specs, arguments, scratch, name, aliases={}):
    pairing = [
        pltpu.VMEM((8, TILE), jnp.int32),
        pltpu.SMEM((8, TILE), jnp.int32),
        pltpu.SMEM((2 * (HELD + BATCH + 1),), jnp.int32),
        pltpu.SMEM((NQ + 1,), jnp.int32),
        pltpu.SMEM((NQ + 1,), jnp.int32),
        pltpu.SemaphoreType.DMA,
    ]
    return pl.pallas_call(
        body,
        out_shape=out_shape,
        in_specs=[pl.BlockSpec(memory_space=space) for _, space in arguments],
        out_specs=out_specs,
        scratch_shapes=pairing + scratch,
        input_output_aliases=aliases,
        compiler_params=pltpu.CompilerParams(vmem_limit_bytes=24 * 2**20),
        cost_estimate=pl.CostEstimate(
            flops=5_000_000_000, bytes_accessed=16_000_000, transcendentals=0
        ),
        name=name,
    )(*(array for array, _ in arguments))


def chosen_part(plan, arrays, chosen, space):
    steps = [step for step in plan if step[0] in chosen]
    return [(step[0] - chosen[0],) + step[1:] for step in steps], [(arrays[i], space) for i in chosen]


IN_VMEM = pl.BlockSpec(memory_space=pltpu.VMEM)
SUMS = [
    jax.ShapeDtypeStruct((32, ROWS, TILE), jnp.bfloat16),
    jax.ShapeDtypeStruct((NQ, ROWS, TILE), jnp.float32),
]


def contract_early(position, tiles, steps, pieces):
    return call(
        functools.partial(first_part, steps, len(pieces)),
        SUMS[1], IN_VMEM,
        [(position, pltpu.SMEM), (tiles, pltpu.VMEM)] + pieces,
        [pltpu.SemaphoreType.DMA, pltpu.VMEM((32, ROWS, TILE), jnp.bfloat16)], "first_part",
    )


def contract_late(position, own, other, first_sums, steps, pieces):
    smem, vmem, dma = pltpu.SMEM, pltpu.VMEM, pltpu.SemaphoreType.DMA
    amps, second_sums = call(
        functools.partial(second_part, steps, len(pieces)),
        SUMS, [IN_VMEM, IN_VMEM],
        [(position, smem), (own, vmem)] + pieces,
        [dma], "second_part",
    )
    return call(
        last_part,
        jax.ShapeDtypeStruct((ROWS, NQ * TILE), jnp.bfloat16),
        pl.BlockSpec(memory_space=pl.ANY),
        [(position, smem), (other, vmem), (amps, vmem), (first_sums, vmem), (second_sums, vmem)],
        [pltpu.VMEM((NQ, ROWS, TILE), jnp.float32), pltpu.VMEM((NQ // SPAN, ROWS, SPAN * TILE), jnp.bfloat16), dma((NQ // SPAN,))],
        "last_part",
    )


def shards(amplitudes, tiles, tile_ids):
    kt = jnp.where(tile_ids >= 0, tile_ids >> 4, -1)
    qt = tile_ids & 15
    ids = jnp.concatenate([kt, qt], axis=0).astype(jnp.bfloat16)
    ids = jnp.pad(ids, ((0, 14), (0, TILE - SLOTS)))
    block = jnp.concatenate([tiles.reshape(SLOTS * TILE, TILE), ids], axis=0)

    block_z = from_row(block, dz=1)
    y_up, y_down = (from_col(amplitudes, dy=dy) for dy in (1, 3))
    first = amplitudes[:ROWS_A]
    z_up, z_down = (from_col(first, dz=dz) for dz in (1, 3))
    block_z, y_up, y_down, z_up, z_down = fence(block_z, y_up, y_down, z_up, z_down)

    x_blocks = [jnp.stack([block, block_z])]
    x_blocks.append(from_row(x_blocks[-1], dx=1))
    y_top, y_low = from_col(y_down[:HALF], dy=3), from_col(y_up[HALF:], dy=1)
    z_top, z_low = from_col(z_down[:HALF_A], dz=3), from_col(z_up[HALF_A:], dz=1)
    x_blocks[-1], y_top, y_low, z_top, z_low = fence(x_blocks[-1], y_top, y_low, z_top, z_low)

    firsts = [jnp.concatenate([z_up, z_down, z_top, z_low], axis=0)]
    lasts = [jnp.concatenate([rows[ROWS_A:] for rows in (amplitudes, y_up, y_down)] + [y_low[ROWS_A - HALF :]], axis=0)]
    x_blocks.append(from_row(x_blocks[-1], dx=1))
    firsts += [from_col(firsts[0], dy=dy) for dy in (1, 3)]
    lasts += [from_col(lasts[0], dz=dz) for dz in (1, 3)]
    x_blocks[-1], firsts[1], firsts[2], lasts[1], lasts[2] = fence(
        x_blocks[-1], firsts[1], firsts[2], lasts[1], lasts[2]
    )

    plan = [(0, 0, ROWS, 0, 0), (1, 0, ROWS, 1, 0), (2, 0, ROWS, 2, 0), (3, 0, HALF, 3, 0)]
    plan.append((4, 0, ROWS - HALF, 3, HALF))
    for i in range(3):
        for j in range(3):
            plan.append((5 + i, j * ROWS_A, ROWS_A, 4 * (j + 1) + i, 0))
    plan += [(10, 0, ROWS_A, 7, 0), (10, ROWS_A, HALF_A, 11, 0)]
    plan += [(11, 0, HALF_A, 11, HALF_A), (11, HALF_A, ROWS_A, 15, 0)]
    for j in range(4):
        plan.append((8, j * ROWS_B, ROWS_B, 4 + j, ROWS_A))
        plan.append((9, j * ROWS_B, ROWS_B, 8 + j, ROWS_A))
        plan.append((12 + j // 2, j % 2 * ROWS_B, ROWS_B, 12 + j, ROWS_A))
    cut, cut_b = 3 * ROWS_A // 2, 2 * ROWS_B
    early_tiles = jnp.concatenate(x_blocks, axis=0)
    x_blocks.append(from_row(x_blocks[-1], dx=1))
    firsts += [from_col(firsts[2][:cut], dy=3), from_col(firsts[1][cut:], dy=1)]
    lasts += [from_col(lasts[2][:cut_b], dz=3), from_col(lasts[1][cut_b:], dz=1)]
    position = jnp.stack([lax.axis_index("col") // 4, lax.axis_index("col") % 4]).astype(jnp.int32)
    arrays = [amplitudes, y_up, y_down, y_top, y_low] + firsts[:3] + lasts[1:3] + firsts[3:] + lasts[3:]
    sums = contract_early(
        position, early_tiles, *chosen_part(plan, arrays, range(10), pl.ANY)
    )
    x_blocks[-1], sums, *arrays[10:] = fence(x_blocks[-1], sums, *arrays[10:])

    own = jnp.concatenate(x_blocks, axis=0)
    other = from_row(own, dcore=1)
    steps, pieces = chosen_part(plan, arrays, range(14), pl.ANY)
    return contract_late(position, own, other, sums, steps, pieces)


def solution(mesh):
    in_specs = (P("row", "col"), P("col", "row", None, None), P("col", "row"))
    out_specs = P("row", "col")
    return jax.shard_map(shards, mesh=mesh, in_specs=in_specs, out_specs=out_specs, check_vma=False)
```

```python
import functools
import itertools

import jax
import jax.numpy as jnp
from jax import lax
from jax.experimental import pallas as pl
from jax.experimental.pallas import tpu as pltpu
from jax.sharding import PartitionSpec as P

TILE = 128
NQ = 16
ROWS = 624
ROWS_A = 480
ROWS_B = ROWS - ROWS_A
HALF = 320
HALF_A = ROWS_A // 2
SLOTS = 8
HELD = 64
EARLY_SLOTS = 48
EARLY = (0, 1, 2, 3, 4, 5, 6, 8, 9, 10)
BATCH = 6
SPAN = 4
EMPTY = -1


def rank_of(d):
    return d ^ (d >> 1)


def fence(*values):
    return lax.optimization_barrier(values)


def from_col(value, dy=0, dz=0):
    perm = [
        ((y + dy) % 4 * 4 + (z + dz) % 4, y * 4 + z) for y in range(4) for z in range(4)
    ]
    return lax.ppermute(value, "col", perm)


def from_row(value, dx=0, dz=0, dcore=0):
    perm = []
    for x, z, core in itertools.product(range(4), range(2), range(2)):
        at_x = (x + dx * (1 - 2 * core)) % 4
        perm.append(((at_x * 2 + (z ^ dz)) * 2 + (core ^ dcore), (x * 2 + z) * 2 + core))
    return lax.ppermute(value, "row", perm)


def pair_tiles(position, tiles, wanted, codes, codes_smem, pairs, last, counts, sem):
    n = tiles.shape[0]
    y, z = position[0], position[1]
    lane = lax.broadcasted_iota(jnp.int32, (1, TILE), 1)
    for i in range(n):
        rows = tiles[i, SLOTS * TILE : SLOTS * TILE + 16, :].astype(jnp.float32)
        kt, qt = rows[0:1].astype(jnp.int32), rows[1:2].astype(jnp.int32)
        owner = kt >> 1
        place = rank_of(((owner & 3) - z) & 3) * 4 + rank_of(((owner >> 2) - y) & 3)
        block = (place * 2 + (kt & 1)) & 31
        slot = i * SLOTS + lane
        live = (kt >= 0) & wanted(slot, block)
        codes[i : i + 1, :] = jnp.where(live, ((qt & 15) * HELD + slot) * 32 + block, EMPTY)
    copy = pltpu.make_async_copy(codes, codes_smem, sem)
    copy.start()
    for q in range(NQ + 1):
        counts[q] = 0
    copy.wait()

    def put(i, n_pairs):
        for j in range(SLOTS):
            code = codes_smem[i, j]
            live = code >= 0
            q = jnp.where(live, code >> 11, NQ)
            count = counts[q]
            opens = (count & 1) == 0
            at = jnp.where(live, jnp.where(opens, n_pairs, last[q]), HELD + BATCH)
            counts[q] = count + 1
            last[q] = at
            pairs[at * 2] = jnp.where(opens, code, pairs[at * 2])
            pairs[at * 2 + 1] = jnp.where(opens, EMPTY, code)
            n_pairs = n_pairs + (live & opens).astype(jnp.int32)
        return n_pairs

    for q in range(NQ + 1):
        last[q] = 0
    n_pairs = lax.fori_loop(0, n, put, jnp.int32(0))
    for i in range(2 * BATCH):
        pairs[n_pairs * 2 + i] = EMPTY
    return n_pairs


def accumulate(n_pairs, pairs, tiles, amps, sums):
    def load(code):
        item = jnp.maximum(code, 0)
        slot = (item >> 5) & (HELD - 1)
        row = pl.ds(pl.multiple_of((slot & 7) * TILE, TILE), TILE)
        tile = tiles[slot >> 3, row, :]
        return amps[item & 31], jnp.where(code >= 0, tile, jnp.zeros_like(tile))

    def step(batch, carry):
        values = []
        for i in range(BATCH):
            at = (batch * BATCH + i) * 2
            (left, upper), (right, lower) = load(pairs[at]), load(pairs[at + 1])
            value = jnp.dot(
                jnp.concatenate([left, right], axis=1),
                jnp.concatenate([upper, lower], axis=0),
                preferred_element_type=jnp.float32,
            )
            values.append((jnp.maximum(pairs[at], 0) >> 11, value))
        for q, value in values:
            sums[q] += value
        return carry

    lax.fori_loop(0, (n_pairs + BATCH - 1) // BATCH, step, 0)


def moves(plan, pieces, amps, sem):
    return [
        pltpu.make_async_copy(
            pieces[ref].at[pl.ds(src, rows), pl.ds(sub * TILE, TILE)],
            amps.at[place * 2 + sub, pl.ds(dst, rows)],
            sem,
        )
        for ref, src, rows, place, dst in plan
        for sub in range(2)
    ]


def early_pair(slot, block):
    early = functools.reduce(jnp.logical_or, [(block >> 1) == place for place in EARLY])
    return (slot < EARLY_SLOTS) & early


def first_part(plan, n_pieces, position, tiles, *refs):
    sums, *pairing, code_sem, sem, amps = refs[n_pieces:]
    copies = moves(plan, refs[:n_pieces], amps, sem)
    for copy in copies:
        copy.start()
    sums[...] = jnp.zeros_like(sums)
    n_pairs = pair_tiles(position, tiles, early_pair, *pairing, code_sem)
    for copy in copies:
        copy.wait()
    accumulate(n_pairs, pairing[2], tiles, amps, sums)


def second_part(plan, n_pieces, position, tiles, *refs):
    amps, sums, *pairing, code_sem, sem = refs[n_pieces:]
    copies = moves(plan, refs[:n_pieces], amps, sem)
    for copy in copies:
        copy.start()
    sums[...] = jnp.zeros_like(sums)

    def wanted(slot, block):
        return jnp.logical_not(early_pair(slot, block))

    n_pairs = pair_tiles(position, tiles, wanted, *pairing, code_sem)
    for copy in copies:
        copy.wait()
    accumulate(n_pairs, pairing[2], tiles, amps, sums)


def last_part(position, tiles, amps, first_sums, second_sums, out, *refs):
    *pairing, code_sem, sums, stage, out_sem = refs
    sums[...] = first_sums[...] + second_sums[...]
    n_pairs = pair_tiles(position, tiles, lambda slot, block: slot >= 0, *pairing, code_sem)
    accumulate(n_pairs, pairing[2], tiles, amps, sums)
    writes = []
    for i in range(NQ // SPAN):
        for j in range(SPAN):
            stage[i, :, j * TILE : (j + 1) * TILE] = sums[i * SPAN + j].astype(jnp.bfloat16)
        columns = pl.ds(i * SPAN * TILE, SPAN * TILE)
        writes.append(pltpu.make_async_copy(stage.at[i], out.at[:, columns], out_sem.at[i]))
        writes[i].start()
    for write in writes:
        write.wait()


def call(body, out_shape, out_specs, arguments, scratch, name, aliases={}):
    pairing = [
        pltpu.VMEM((8, TILE), jnp.int32),
        pltpu.SMEM((8, TILE), jnp.int32),
        pltpu.SMEM((2 * (HELD + BATCH + 1),), jnp.int32),
        pltpu.SMEM((NQ + 1,), jnp.int32),
        pltpu.SMEM((NQ + 1,), jnp.int32),
        pltpu.SemaphoreType.DMA,
    ]
    return pl.pallas_call(
        body,
        out_shape=out_shape,
        in_specs=[pl.BlockSpec(memory_space=space) for _, space in arguments],
        out_specs=out_specs,
        scratch_shapes=pairing + scratch,
        input_output_aliases=aliases,
        compiler_params=pltpu.CompilerParams(vmem_limit_bytes=24 * 2**20),
        cost_estimate=pl.CostEstimate(
            flops=5_000_000_000, bytes_accessed=16_000_000, transcendentals=0
        ),
        name=name,
    )(*(array for array, _ in arguments))


def chosen_part(plan, arrays, chosen, space):
    steps = [step for step in plan if step[0] in chosen]
    return [(step[0] - chosen[0],) + step[1:] for step in steps], [(arrays[i], space) for i in chosen]


IN_VMEM = pl.BlockSpec(memory_space=pltpu.VMEM)
SUMS = [
    jax.ShapeDtypeStruct((32, ROWS, TILE), jnp.bfloat16),
    jax.ShapeDtypeStruct((NQ, ROWS, TILE), jnp.float32),
]


def contract_early(position, tiles, steps, pieces):
    return call(
        functools.partial(first_part, steps, len(pieces)),
        SUMS[1], IN_VMEM,
        [(position, pltpu.SMEM), (tiles, pltpu.VMEM)] + pieces,
        [pltpu.SemaphoreType.DMA, pltpu.VMEM((32, ROWS, TILE), jnp.bfloat16)], "first_part",
    )


def contract_late(position, own, other, first_sums, steps, pieces):
    smem, vmem, dma = pltpu.SMEM, pltpu.VMEM, pltpu.SemaphoreType.DMA
    amps, second_sums = call(
        functools.partial(second_part, steps, len(pieces)),
        SUMS, [IN_VMEM, IN_VMEM],
        [(position, smem), (own, vmem)] + pieces,
        [dma], "second_part",
    )
    return call(
        last_part,
        jax.ShapeDtypeStruct((ROWS, NQ * TILE), jnp.bfloat16),
        pl.BlockSpec(memory_space=pl.ANY),
        [(position, smem), (other, vmem), (amps, vmem), (first_sums, vmem), (second_sums, vmem)],
        [pltpu.VMEM((NQ, ROWS, TILE), jnp.float32), pltpu.VMEM((NQ // SPAN, ROWS, SPAN * TILE), jnp.bfloat16), dma((NQ // SPAN,))],
        "last_part",
    )


def shards(amplitudes, tiles, tile_ids):
    kt = jnp.where(tile_ids >= 0, tile_ids >> 4, -1)
    qt = tile_ids & 15
    ids = jnp.concatenate([kt, qt], axis=0).astype(jnp.bfloat16)
    ids = jnp.pad(ids, ((0, 14), (0, TILE - SLOTS)))
    block = jnp.concatenate([tiles.reshape(SLOTS * TILE, TILE), ids], axis=0)

    block_z = from_row(block, dz=1)
    y_up, y_down = (from_col(amplitudes, dy=dy) for dy in (1, 3))
    first = amplitudes[:ROWS_A]
    z_up, z_down = (from_col(first, dz=dz) for dz in (1, 3))
    both = jnp.stack([block, block_z])
    near = jnp.concatenate([z_up, z_down], axis=0)
    both, y_up, y_down, near = fence(both, y_up, y_down, near)

    x_blocks = [both]
    x_blocks.append(from_row(x_blocks[-1], dx=1))
    y_top, y_low = from_col(y_down[:HALF], dy=3), from_col(y_up[HALF:], dy=1)
    z_top, z_low = from_col(near[ROWS_A : ROWS_A + HALF_A], dz=3), from_col(near[HALF_A:ROWS_A], dz=1)
    firsts = [jnp.concatenate([near, z_top, z_low], axis=0)]
    x_blocks[-1], y_top, y_low, firsts[0] = fence(x_blocks[-1], y_top, y_low, firsts[0])

    lasts = [jnp.concatenate([rows[ROWS_A:] for rows in (amplitudes, y_up, y_down)] + [y_low[ROWS_A - HALF :]], axis=0)]
    x_blocks.append(from_row(x_blocks[-1], dx=1))
    firsts += [from_col(firsts[0], dy=dy) for dy in (1, 3)]
    lasts += [from_col(lasts[0], dz=dz) for dz in (1, 3)]

    plan = [(0, 0, ROWS, 0, 0), (1, 0, ROWS, 1, 0), (2, 0, ROWS, 2, 0), (3, 0, HALF, 3, 0)]
    plan.append((4, 0, ROWS - HALF, 3, HALF))
    for i in range(3):
        for j in range(3):
            plan.append((5 + i, j * ROWS_A, ROWS_A, 4 * (j + 1) + i, 0))
    plan += [(10, 0, ROWS_A, 7, 0), (10, ROWS_A, HALF_A, 11, 0)]
    plan += [(11, 0, HALF_A, 11, HALF_A), (11, HALF_A, ROWS_A, 15, 0)]
    for j in range(4):
        plan.append((8, j * ROWS_B, ROWS_B, 4 + j, ROWS_A))
        plan.append((9, j * ROWS_B, ROWS_B, 8 + j, ROWS_A))
        plan.append((12 + j // 2, j % 2 * ROWS_B, ROWS_B, 12 + j, ROWS_A))
    cut, cut_b = 3 * ROWS_A // 2, 2 * ROWS_B
    early_tiles = jnp.concatenate(x_blocks, axis=0)
    x_blocks.append(from_row(x_blocks[-1], dx=1))
    firsts += [from_col(firsts[2][:cut], dy=3), from_col(firsts[1][cut:], dy=1)]
    lasts += [from_col(lasts[2][:cut_b], dz=3), from_col(lasts[1][cut_b:], dz=1)]
    position = jnp.stack([lax.axis_index("col") // 4, lax.axis_index("col") % 4]).astype(jnp.int32)
    arrays = [amplitudes, y_up, y_down, y_top, y_low] + firsts[:3] + lasts[1:3] + firsts[3:] + lasts[3:]
    sums = contract_early(
        position, early_tiles, *chosen_part(plan, arrays, range(10), pl.ANY)
    )
    x_blocks[-1], sums, *arrays[10:] = fence(x_blocks[-1], sums, *arrays[10:])

    own = jnp.concatenate(x_blocks, axis=0)
    other = from_row(own, dcore=1)
    steps, pieces = chosen_part(plan, arrays, range(14), pl.ANY)
    return contract_late(position, own, other, sums, steps, pieces)


def solution(mesh):
    in_specs = (P("row", "col"), P("col", "row", None, None), P("col", "row"))
    out_specs = P("row", "col")
    return jax.shard_map(shards, mesh=mesh, in_specs=in_specs, out_specs=out_specs, check_vma=False)
```

```python
import functools
import itertools

import jax
import jax.numpy as jnp
from jax import lax
from jax.experimental import pallas as pl
from jax.experimental.pallas import tpu as pltpu
from jax.sharding import PartitionSpec as P

TILE = 128
NQ = 16
ROWS = 624
ROWS_A = 480
ROWS_B = ROWS - ROWS_A
HALF = 320
HALF_A = ROWS_A // 2
SLOTS = 8
HELD = 64
EARLY_SLOTS = 48
EARLY = (0, 1, 2, 3, 4, 5, 6, 8, 9, 10)
BATCH = 6
SPAN = 4
EMPTY = -1


def rank_of(d):
    return d ^ (d >> 1)


def fence(*values):
    return lax.optimization_barrier(values)


def from_col(value, dy=0, dz=0):
    perm = [
        ((y + dy) % 4 * 4 + (z + dz) % 4, y * 4 + z) for y in range(4) for z in range(4)
    ]
    return lax.ppermute(value, "col", perm)


def from_row(value, dx=0, dz=0, dcore=0):
    perm = []
    for x, z, core in itertools.product(range(4), range(2), range(2)):
        at_x = (x + dx * (1 - 2 * core)) % 4
        perm.append(((at_x * 2 + (z ^ dz)) * 2 + (core ^ dcore), (x * 2 + z) * 2 + core))
    return lax.ppermute(value, "row", perm)


def pair_tiles(position, tiles, wanted, meanwhile, codes, codes_smem, pairs, last, counts, sem):
    n = tiles.shape[0]
    y, z = position[0], position[1]
    lane = lax.broadcasted_iota(jnp.int32, (1, TILE), 1)
    for i in range(n):
        rows = tiles[i, SLOTS * TILE : SLOTS * TILE + 16, :].astype(jnp.float32)
        kt, qt = rows[0:1].astype(jnp.int32), rows[1:2].astype(jnp.int32)
        owner = kt >> 1
        place = rank_of(((owner & 3) - z) & 3) * 4 + rank_of(((owner >> 2) - y) & 3)
        block = (place * 2 + (kt & 1)) & 31
        slot = i * SLOTS + lane
        live = (kt >= 0) & wanted(slot, block)
        codes[i : i + 1, :] = jnp.where(live, ((qt & 15) * HELD + slot) * 32 + block, EMPTY)
    copy = pltpu.make_async_copy(codes, codes_smem, sem)
    copy.start()
    for q in range(NQ + 1):
        counts[q] = 0
        last[q] = 0
    meanwhile()
    copy.wait()

    def put(i, n_pairs):
        for j in range(SLOTS):
            code = codes_smem[i, j]
            live = code >= 0
            q = jnp.where(live, code >> 11, NQ)
            count = counts[q]
            opens = (count & 1) == 0
            at = jnp.where(live, jnp.where(opens, n_pairs, last[q]), HELD + BATCH)
            counts[q] = count + 1
            last[q] = at
            pairs[at * 2] = jnp.where(opens, code, pairs[at * 2])
            pairs[at * 2 + 1] = jnp.where(opens, EMPTY, code)
            n_pairs = n_pairs + (live & opens).astype(jnp.int32)
        return n_pairs

    n_pairs = lax.fori_loop(0, n, put, jnp.int32(0))
    for i in range(2 * BATCH):
        pairs[n_pairs * 2 + i] = EMPTY
    return n_pairs


def accumulate(n_pairs, pairs, tiles, amps, sums):
    def load(code):
        item = jnp.maximum(code, 0)
        slot = (item >> 5) & (HELD - 1)
        row = pl.ds(pl.multiple_of((slot & 7) * TILE, TILE), TILE)
        tile = tiles[slot >> 3, row, :]
        return amps[item & 31], jnp.where(code >= 0, tile, jnp.zeros_like(tile))

    def step(batch, carry):
        values = []
        for i in range(BATCH):
            at = (batch * BATCH + i) * 2
            (left, upper), (right, lower) = load(pairs[at]), load(pairs[at + 1])
            value = jnp.dot(
                jnp.concatenate([left, right], axis=1),
                jnp.concatenate([upper, lower], axis=0),
                preferred_element_type=jnp.float32,
            )
            values.append((jnp.maximum(pairs[at], 0) >> 11, value))
        for q, value in values:
            sums[q] += value
        return carry

    lax.fori_loop(0, (n_pairs + BATCH - 1) // BATCH, step, 0)


def moves(plan, pieces, amps, sem):
    return [
        pltpu.make_async_copy(
            pieces[ref].at[pl.ds(src, rows), pl.ds(sub * TILE, TILE)],
            amps.at[place * 2 + sub, pl.ds(dst, rows)],
            sem,
        )
        for ref, src, rows, place, dst in plan
        for sub in range(2)
    ]


def early_pair(slot, block):
    early = functools.reduce(jnp.logical_or, [(block >> 1) == place for place in EARLY])
    return (slot < EARLY_SLOTS) & early


def first_part(plan, n_pieces, position, tiles, *refs):
    sums, *pairing, code_sem, sem, amps = refs[n_pieces:]
    copies = moves(plan, refs[:n_pieces], amps, sem)
    for copy in copies:
        copy.start()

    def clear():
        sums[...] = jnp.zeros_like(sums)

    n_pairs = pair_tiles(position, tiles, early_pair, clear, *pairing, code_sem)
    for copy in copies:
        copy.wait()
    accumulate(n_pairs, pairing[2], tiles, amps, sums)


def second_part(plan, n_pieces, position, tiles, *refs):
    amps, sums, *pairing, code_sem, sem = refs[n_pieces:]
    copies = moves(plan, refs[:n_pieces], amps, sem)
    for copy in copies:
        copy.start()

    def wanted(slot, block):
        return jnp.logical_not(early_pair(slot, block))

    def clear():
        sums[...] = jnp.zeros_like(sums)

    n_pairs = pair_tiles(position, tiles, wanted, clear, *pairing, code_sem)
    for copy in copies:
        copy.wait()
    accumulate(n_pairs, pairing[2], tiles, amps, sums)


def last_part(position, tiles, amps, first_sums, second_sums, out, *refs):
    *pairing, code_sem, sums, stage, out_sem = refs

    def add():
        sums[...] = first_sums[...] + second_sums[...]

    n_pairs = pair_tiles(position, tiles, lambda slot, block: slot >= 0, add, *pairing, code_sem)
    accumulate(n_pairs, pairing[2], tiles, amps, sums)
    writes = []
    for i in range(NQ // SPAN):
        for j in range(SPAN):
            stage[i, :, j * TILE : (j + 1) * TILE] = sums[i * SPAN + j].astype(jnp.bfloat16)
        columns = pl.ds(i * SPAN * TILE, SPAN * TILE)
        writes.append(pltpu.make_async_copy(stage.at[i], out.at[:, columns], out_sem.at[i]))
        writes[i].start()
    for write in writes:
        write.wait()


def call(body, out_shape, out_specs, arguments, scratch, name, aliases={}):
    pairing = [
        pltpu.VMEM((8, TILE), jnp.int32),
        pltpu.SMEM((8, TILE), jnp.int32),
        pltpu.SMEM((2 * (HELD + BATCH + 1),), jnp.int32),
        pltpu.SMEM((NQ + 1,), jnp.int32),
        pltpu.SMEM((NQ + 1,), jnp.int32),
        pltpu.SemaphoreType.DMA,
    ]
    return pl.pallas_call(
        body,
        out_shape=out_shape,
        in_specs=[pl.BlockSpec(memory_space=space) for _, space in arguments],
        out_specs=out_specs,
        scratch_shapes=pairing + scratch,
        input_output_aliases=aliases,
        compiler_params=pltpu.CompilerParams(vmem_limit_bytes=24 * 2**20),
        cost_estimate=pl.CostEstimate(
            flops=5_000_000_000, bytes_accessed=16_000_000, transcendentals=0
        ),
        name=name,
    )(*(array for array, _ in arguments))


def chosen_part(plan, arrays, chosen, space):
    steps = [step for step in plan if step[0] in chosen]
    return [(step[0] - chosen[0],) + step[1:] for step in steps], [(arrays[i], space) for i in chosen]


IN_VMEM = pl.BlockSpec(memory_space=pltpu.VMEM)
SUMS = [
    jax.ShapeDtypeStruct((32, ROWS, TILE), jnp.bfloat16),
    jax.ShapeDtypeStruct((NQ, ROWS, TILE), jnp.float32),
]


def contract_early(position, tiles, steps, pieces):
    return call(
        functools.partial(first_part, steps, len(pieces)),
        SUMS[1], IN_VMEM,
        [(position, pltpu.SMEM), (tiles, pltpu.VMEM)] + pieces,
        [pltpu.SemaphoreType.DMA, pltpu.VMEM((32, ROWS, TILE), jnp.bfloat16)], "first_part",
    )


def contract_late(position, own, other, first_sums, steps, pieces):
    smem, vmem, dma = pltpu.SMEM, pltpu.VMEM, pltpu.SemaphoreType.DMA
    amps, second_sums = call(
        functools.partial(second_part, steps, len(pieces)),
        SUMS, [IN_VMEM, IN_VMEM],
        [(position, smem), (own, vmem)] + pieces,
        [dma], "second_part",
    )
    return call(
        last_part,
        jax.ShapeDtypeStruct((ROWS, NQ * TILE), jnp.bfloat16),
        pl.BlockSpec(memory_space=pl.ANY),
        [(position, smem), (other, vmem), (amps, vmem), (first_sums, vmem), (second_sums, vmem)],
        [pltpu.VMEM((NQ, ROWS, TILE), jnp.float32), pltpu.VMEM((NQ // SPAN, ROWS, SPAN * TILE), jnp.bfloat16), dma((NQ // SPAN,))],
        "last_part",
    )


def shards(amplitudes, tiles, tile_ids):
    kt = jnp.where(tile_ids >= 0, tile_ids >> 4, -1)
    qt = tile_ids & 15
    ids = jnp.concatenate([kt, qt], axis=0).astype(jnp.bfloat16)
    ids = jnp.pad(ids, ((0, 14), (0, TILE - SLOTS)))
    block = jnp.concatenate([tiles.reshape(SLOTS * TILE, TILE), ids], axis=0)

    block_z = from_row(block, dz=1)
    y_up, y_down = (from_col(amplitudes, dy=dy) for dy in (1, 3))
    first = amplitudes[:ROWS_A]
    z_up, z_down = (from_col(first, dz=dz) for dz in (1, 3))
    both = jnp.stack([block, block_z])
    near = jnp.concatenate([z_up, z_down], axis=0)
    both, near = fence(both, near)

    x_blocks = [both]
    x_blocks.append(from_row(x_blocks[-1], dx=1))
    y_top, y_low = from_col(y_down[:HALF], dy=3), from_col(y_up[HALF:], dy=1)
    z_top, z_low = from_col(near[ROWS_A : ROWS_A + HALF_A], dz=3), from_col(near[HALF_A:ROWS_A], dz=1)
    firsts = [jnp.concatenate([near, z_top, z_low], axis=0)]
    x_blocks[-1], y_top, y_low, firsts[0] = fence(x_blocks[-1], y_top, y_low, firsts[0])

    lasts = [jnp.concatenate([rows[ROWS_A:] for rows in (amplitudes, y_up, y_down)] + [y_low[ROWS_A - HALF :]], axis=0)]
    x_blocks.append(from_row(x_blocks[-1], dx=1))
    firsts += [from_col(firsts[0], dy=dy) for dy in (1, 3)]
    lasts += [from_col(lasts[0], dz=dz) for dz in (1, 3)]

    x_blocks[-1], lasts[1], lasts[2] = fence(x_blocks[-1], lasts[1], lasts[2])

    plan = [(0, 0, ROWS, 0, 0), (1, 0, ROWS, 1, 0), (2, 0, ROWS, 2, 0), (3, 0, HALF, 3, 0)]
    plan.append((4, 0, ROWS - HALF, 3, HALF))
    for i in range(3):
        for j in range(3):
            plan.append((5 + i, j * ROWS_A, ROWS_A, 4 * (j + 1) + i, 0))
    plan += [(10, 0, ROWS_A, 7, 0), (10, ROWS_A, HALF_A, 11, 0)]
    plan += [(11, 0, HALF_A, 11, HALF_A), (11, HALF_A, ROWS_A, 15, 0)]
    for j in range(4):
        plan.append((8, j * ROWS_B, ROWS_B, 4 + j, ROWS_A))
        plan.append((9, j * ROWS_B, ROWS_B, 8 + j, ROWS_A))
        plan.append((12 + j // 2, j % 2 * ROWS_B, ROWS_B, 12 + j, ROWS_A))
    cut, cut_b = 3 * ROWS_A // 2, 2 * ROWS_B
    early_tiles = jnp.concatenate(x_blocks, axis=0)
    x_blocks.append(from_row(x_blocks[-1], dx=1))
    firsts += [from_col(firsts[2][:cut], dy=3), from_col(firsts[1][cut:], dy=1)]
    lasts += [from_col(lasts[2][:cut_b], dz=3), from_col(lasts[1][cut_b:], dz=1)]
    position = jnp.stack([lax.axis_index("col") // 4, lax.axis_index("col") % 4]).astype(jnp.int32)
    arrays = [amplitudes, y_up, y_down, y_top, y_low] + firsts[:3] + lasts[1:3] + firsts[3:] + lasts[3:]
    sums = contract_early(
        position, early_tiles, *chosen_part(plan, arrays, range(10), pl.ANY)
    )
    x_blocks[-1], sums, *arrays[10:] = fence(x_blocks[-1], sums, *arrays[10:])

    own = jnp.concatenate(x_blocks, axis=0)
    other = from_row(own, dcore=1)
    steps, pieces = chosen_part(plan, arrays, range(14), pl.ANY)
    return contract_late(position, own, other, sums, steps, pieces)


def solution(mesh):
    in_specs = (P("row", "col"), P("col", "row", None, None), P("col", "row"))
    out_specs = P("row", "col")
    return jax.shard_map(shards, mesh=mesh, in_specs=in_specs, out_specs=out_specs, check_vma=False)
```

```python
import functools
import itertools

import jax
import jax.numpy as jnp
from jax import lax
from jax.experimental import pallas as pl
from jax.experimental.pallas import tpu as pltpu
from jax.sharding import PartitionSpec as P

TILE = 128
NQ = 16
ROWS = 624
ROWS_A = 480
ROWS_B = ROWS - ROWS_A
HALF = 320
HALF_A = ROWS_A // 2
SLOTS = 8
HELD = 64
EARLY_SLOTS = 48
EARLY = (0, 1, 2, 3, 4, 5, 6, 8, 9, 10)
BATCH = 6
SPAN = 4
EMPTY = -1
SECOND = 64 + BATCH


def rank_of(d):
    return d ^ (d >> 1)


def fence(*values):
    return lax.optimization_barrier(values)


def from_col(value, dy=0, dz=0):
    perm = [
        ((y + dy) % 4 * 4 + (z + dz) % 4, y * 4 + z) for y in range(4) for z in range(4)
    ]
    return lax.ppermute(value, "col", perm)


def from_row(value, dx=0, dz=0, dcore=0):
    perm = []
    for x, z, core in itertools.product(range(4), range(2), range(2)):
        at_x = (x + dx * (1 - 2 * core)) % 4
        perm.append(((at_x * 2 + (z ^ dz)) * 2 + (core ^ dcore), (x * 2 + z) * 2 + core))
    return lax.ppermute(value, "row", perm)


def pair_tiles(position, tiles, wanted, meanwhile, split, codes, codes_smem, pairs, last, counts, sem):
    n = tiles.shape[0]
    y, z = position[0], position[1]
    lane = lax.broadcasted_iota(jnp.int32, (1, TILE), 1)
    for i in range(n):
        rows = tiles[i, SLOTS * TILE : SLOTS * TILE + 16, :].astype(jnp.float32)
        kt, qt = rows[0:1].astype(jnp.int32), rows[1:2].astype(jnp.int32)
        owner = kt >> 1
        place = rank_of(((owner & 3) - z) & 3) * 4 + rank_of(((owner >> 2) - y) & 3)
        block = (place * 2 + (kt & 1)) & 31
        slot = i * SLOTS + lane
        live = (kt >= 0) & wanted(slot, block)
        codes[i : i + 1, :] = jnp.where(live, ((qt & 15) * HELD + slot) * 32 + block, EMPTY)
    copy = pltpu.make_async_copy(codes, codes_smem, sem)
    copy.start()
    for q in range(NQ + 1):
        counts[q] = 0
        last[q] = 0
    meanwhile()
    copy.wait()

    def put(i, n_pairs):
        low, high = n_pairs
        for j in range(SLOTS):
            code = codes_smem[i, j]
            live = code >= 0
            q = jnp.where(live, code >> 11, NQ)
            count = counts[q]
            opens = (count & 1) == 0
            at = jnp.where(live, jnp.where(opens, jnp.where(q < split, low, SECOND + high), last[q]), 2 * SECOND)
            counts[q] = count + 1
            last[q] = at
            pairs[at * 2] = jnp.where(opens, code, pairs[at * 2])
            pairs[at * 2 + 1] = jnp.where(opens, EMPTY, code)
            new = (live & opens).astype(jnp.int32)
            low = low + jnp.where(q < split, new, 0)
            high = high + jnp.where(q < split, 0, new)
        return low, high

    low, high = lax.fori_loop(0, n, put, (jnp.int32(0), jnp.int32(0)))
    for i in range(2 * BATCH):
        pairs[low * 2 + i] = EMPTY
        pairs[(SECOND + high) * 2 + i] = EMPTY
    return low, high


def accumulate(n_pairs, pairs, tiles, amps, sums, first=0):
    def load(code):
        item = jnp.maximum(code, 0)
        slot = (item >> 5) & (HELD - 1)
        row = pl.ds(pl.multiple_of((slot & 7) * TILE, TILE), TILE)
        tile = tiles[slot >> 3, row, :]
        return amps[item & 31], jnp.where(code >= 0, tile, jnp.zeros_like(tile))

    def step(batch, carry):
        values = []
        for i in range(BATCH):
            at = (first + batch * BATCH + i) * 2
            (left, upper), (right, lower) = load(pairs[at]), load(pairs[at + 1])
            value = jnp.dot(
                jnp.concatenate([left, right], axis=1),
                jnp.concatenate([upper, lower], axis=0),
                preferred_element_type=jnp.float32,
            )
            values.append((jnp.maximum(pairs[at], 0) >> 11, value))
        for q, value in values:
            sums[q] += value
        return carry

    lax.fori_loop(0, (n_pairs + BATCH - 1) // BATCH, step, 0)


def moves(plan, pieces, amps, sem):
    return [
        pltpu.make_async_copy(
            pieces[ref].at[pl.ds(src, rows), pl.ds(sub * TILE, TILE)],
            amps.at[place * 2 + sub, pl.ds(dst, rows)],
            sem,
        )
        for ref, src, rows, place, dst in plan
        for sub in range(2)
    ]


def early_pair(slot, block):
    early = functools.reduce(jnp.logical_or, [(block >> 1) == place for place in EARLY])
    return (slot < EARLY_SLOTS) & early


def first_part(plan, n_pieces, position, tiles, *refs):
    sums, *pairing, code_sem, sem, amps = refs[n_pieces:]
    copies = moves(plan, refs[:n_pieces], amps, sem)
    for copy in copies:
        copy.start()

    def clear():
        sums[...] = jnp.zeros_like(sums)

    n_pairs, _ = pair_tiles(position, tiles, early_pair, clear, NQ, *pairing, code_sem)
    for copy in copies:
        copy.wait()
    accumulate(n_pairs, pairing[2], tiles, amps, sums)


def second_part(plan, n_pieces, position, tiles, *refs):
    amps, sums, *pairing, code_sem, sem = refs[n_pieces:]
    copies = moves(plan, refs[:n_pieces], amps, sem)
    for copy in copies:
        copy.start()

    def wanted(slot, block):
        return jnp.logical_not(early_pair(slot, block))

    def clear():
        sums[...] = jnp.zeros_like(sums)

    n_pairs, _ = pair_tiles(position, tiles, wanted, clear, NQ, *pairing, code_sem)
    for copy in copies:
        copy.wait()
    accumulate(n_pairs, pairing[2], tiles, amps, sums)


def last_part(position, tiles, amps, first_sums, second_sums, out, *refs):
    *pairing, code_sem, sums, stage, out_sem = refs

    def add():
        sums[...] = first_sums[...] + second_sums[...]

    low, high = pair_tiles(position, tiles, lambda slot, block: slot >= 0, add, NQ // 2, *pairing, code_sem)
    accumulate(low, pairing[2], tiles, amps, sums)
    writes = []
    for i in range(NQ // SPAN):
        if i * SPAN == NQ // 2:
            accumulate(high, pairing[2], tiles, amps, sums, SECOND)
        for j in range(SPAN):
            stage[i, :, j * TILE : (j + 1) * TILE] = sums[i * SPAN + j].astype(jnp.bfloat16)
        columns = pl.ds(i * SPAN * TILE, SPAN * TILE)
        writes.append(pltpu.make_async_copy(stage.at[i], out.at[:, columns], out_sem.at[i]))
        writes[i].start()
    for write in writes:
        write.wait()


def call(body, out_shape, out_specs, arguments, scratch, name, aliases={}):
    pairing = [
        pltpu.VMEM((8, TILE), jnp.int32),
        pltpu.SMEM((8, TILE), jnp.int32),
        pltpu.SMEM((4 * SECOND + 2,), jnp.int32),
        pltpu.SMEM((NQ + 1,), jnp.int32),
        pltpu.SMEM((NQ + 1,), jnp.int32),
        pltpu.SemaphoreType.DMA,
    ]
    return pl.pallas_call(
        body,
        out_shape=out_shape,
        in_specs=[pl.BlockSpec(memory_space=space) for _, space in arguments],
        out_specs=out_specs,
        scratch_shapes=pairing + scratch,
        input_output_aliases=aliases,
        compiler_params=pltpu.CompilerParams(vmem_limit_bytes=24 * 2**20),
        cost_estimate=pl.CostEstimate(
            flops=5_000_000_000, bytes_accessed=16_000_000, transcendentals=0
        ),
        name=name,
    )(*(array for array, _ in arguments))


def chosen_part(plan, arrays, chosen, space):
    steps = [step for step in plan if step[0] in chosen]
    return [(step[0] - chosen[0],) + step[1:] for step in steps], [(arrays[i], space) for i in chosen]


IN_VMEM = pl.BlockSpec(memory_space=pltpu.VMEM)
SUMS = [
    jax.ShapeDtypeStruct((32, ROWS, TILE), jnp.bfloat16),
    jax.ShapeDtypeStruct((NQ, ROWS, TILE), jnp.float32),
]


def contract_early(position, tiles, steps, pieces):
    return call(
        functools.partial(first_part, steps, len(pieces)),
        SUMS[1], IN_VMEM,
        [(position, pltpu.SMEM), (tiles, pltpu.VMEM)] + pieces,
        [pltpu.SemaphoreType.DMA, pltpu.VMEM((32, ROWS, TILE), jnp.bfloat16)], "first_part",
    )


def contract_late(position, own, other, first_sums, steps, pieces):
    smem, vmem, dma = pltpu.SMEM, pltpu.VMEM, pltpu.SemaphoreType.DMA
    amps, second_sums = call(
        functools.partial(second_part, steps, len(pieces)),
        SUMS, [IN_VMEM, IN_VMEM],
        [(position, smem), (own, vmem)] + pieces,
        [dma], "second_part",
    )
    return call(
        last_part,
        jax.ShapeDtypeStruct((ROWS, NQ * TILE), jnp.bfloat16),
        pl.BlockSpec(memory_space=pl.ANY),
        [(position, smem), (other, vmem), (amps, vmem), (first_sums, vmem), (second_sums, vmem)],
        [pltpu.VMEM((NQ, ROWS, TILE), jnp.float32), pltpu.VMEM((NQ // SPAN, ROWS, SPAN * TILE), jnp.bfloat16), dma((NQ // SPAN,))],
        "last_part",
    )


def shards(amplitudes, tiles, tile_ids):
    kt = jnp.where(tile_ids >= 0, tile_ids >> 4, -1)
    qt = tile_ids & 15
    ids = jnp.concatenate([kt, qt], axis=0).astype(jnp.bfloat16)
    ids = jnp.pad(ids, ((0, 14), (0, TILE - SLOTS)))
    block = jnp.concatenate([tiles.reshape(SLOTS * TILE, TILE), ids], axis=0)

    block_z = from_row(block, dz=1)
    y_up, y_down = (from_col(amplitudes, dy=dy) for dy in (1, 3))
    first = amplitudes[:ROWS_A]
    z_up, z_down = (from_col(first, dz=dz) for dz in (1, 3))
    both = jnp.stack([block, block_z])
    near = jnp.concatenate([z_up, z_down], axis=0)
    both, near = fence(both, near)

    x_blocks = [both]
    x_blocks.append(from_row(x_blocks[-1], dx=1))
    y_top, y_low = from_col(y_down[:HALF], dy=3), from_col(y_up[HALF:], dy=1)
    z_top, z_low = from_col(near[ROWS_A : ROWS_A + HALF_A], dz=3), from_col(near[HALF_A:ROWS_A], dz=1)
    firsts = [jnp.concatenate([near, z_top, z_low], axis=0)]
    x_blocks[-1], y_top, y_low, firsts[0] = fence(x_blocks[-1], y_top, y_low, firsts[0])

    lasts = [jnp.concatenate([rows[ROWS_A:] for rows in (amplitudes, y_up, y_down)] + [y_low[ROWS_A - HALF :]], axis=0)]
    x_blocks.append(from_row(x_blocks[-1], dx=1))
    firsts += [from_col(firsts[0], dy=dy) for dy in (1, 3)]
    lasts += [from_col(lasts[0], dz=dz) for dz in (1, 3)]

    x_blocks[-1], lasts[1], lasts[2] = fence(x_blocks[-1], lasts[1], lasts[2])

    plan = [(0, 0, ROWS, 0, 0), (1, 0, ROWS, 1, 0), (2, 0, ROWS, 2, 0), (3, 0, HALF, 3, 0)]
    plan.append((4, 0, ROWS - HALF, 3, HALF))
    for i in range(3):
        for j in range(3):
            plan.append((5 + i, j * ROWS_A, ROWS_A, 4 * (j + 1) + i, 0))
    plan += [(10, 0, ROWS_A, 7, 0), (10, ROWS_A, HALF_A, 11, 0)]
    plan += [(11, 0, HALF_A, 11, HALF_A), (11, HALF_A, ROWS_A, 15, 0)]
    for j in range(4):
        plan.append((8, j * ROWS_B, ROWS_B, 4 + j, ROWS_A))
        plan.append((9, j * ROWS_B, ROWS_B, 8 + j, ROWS_A))
        plan.append((12 + j // 2, j % 2 * ROWS_B, ROWS_B, 12 + j, ROWS_A))
    cut, cut_b = 3 * ROWS_A // 2, 2 * ROWS_B
    early_tiles = jnp.concatenate(x_blocks, axis=0)
    x_blocks.append(from_row(x_blocks[-1], dx=1))
    firsts += [from_col(firsts[2][:cut], dy=3), from_col(firsts[1][cut:], dy=1)]
    lasts += [from_col(lasts[2][:cut_b], dz=3), from_col(lasts[1][cut_b:], dz=1)]
    position = jnp.stack([lax.axis_index("col") // 4, lax.axis_index("col") % 4]).astype(jnp.int32)
    arrays = [amplitudes, y_up, y_down, y_top, y_low] + firsts[:3] + lasts[1:3] + firsts[3:] + lasts[3:]
    sums = contract_early(
        position, early_tiles, *chosen_part(plan, arrays, range(10), pl.ANY)
    )
    x_blocks[-1], sums, *arrays[10:] = fence(x_blocks[-1], sums, *arrays[10:])

    own = jnp.concatenate(x_blocks, axis=0)
    other = from_row(own, dcore=1)
    steps, pieces = chosen_part(plan, arrays, range(14), pl.ANY)
    return contract_late(position, own, other, sums, steps, pieces)


def solution(mesh):
    in_specs = (P("row", "col"), P("col", "row", None, None), P("col", "row"))
    out_specs = P("row", "col")
    return jax.shard_map(shards, mesh=mesh, in_specs=in_specs, out_specs=out_specs, check_vma=False)
```
